32 devices in a mesh: clip: 2 (over y), tm: 4 (over z), band: 2 (over x), head: 2 (over core).
Axes of the slice: x: 2, y: 2, z: 4, core: 2. Of those that a mesh axis runs over, the one named last changes fastest.
Arguments:
- queries: bfloat16 [8, 2, 256, 1536], P(('clip', 'tm'), 'band', None, 'head'), parts along dimension 0, may hold values from -6 to 6
- keys: bfloat16 [8, 2, 256, 1536], P(('clip', 'tm'), 'band', None, 'head'), parts along dimension 0, may hold values from -6 to 6
- values: bfloat16 [8, 2, 256, 1536], P(('clip', 'tm'), 'band', None, 'head'), parts along dimension 0, may hold values from -6 to 6
- adj_mask: int32 [8, 2, 2, 2], P(('clip', 'tm'), 'band'), parts along dimension 0, may hold values from 0 to 1, as said below
- border_blocks: int32 [8, 2, 2, 1], P(('clip', 'tm'), 'band'), parts along dimension 0, may hold values from 0 to 1
Outputs:
- attended: bfloat16 [8, 2, 256, 1536], P(('clip', 'tm'), 'band', None, 'head'), parts along dimension 0
The draws below stay inside these ranges and needn't reach their ends.
There are 2 independent parts, one for each index of `clip`. The reference program is written for one: setup_inputs(seed, part) draws one part's arguments, and reference() takes and returns one part's arrays. A program takes and returns all parts, laid end to end along the dimension named above; each array names one. Nothing has to cross between parts.
Inputs may be any that keep to these rules, and one draw needn't show every extreme that they name: `adj_mask`: for each slab, band and direction exactly 1 of the 2 entries are 1.
All inputs are finite; a program needn't handle non-finite values.
Results may differ from the reference program's by a relative error of at most 0.0043.
Values may be sent and summed in bfloat16 or wider, within the bound.
No kernel may reach another device: no remote copies, remote signals or barrier semaphores. Data moves between devices by JAX's collectives and lax.ppermute only.
A program may use at most 64 MiB of HBM per device.

```python
import math
import jax
import jax.numpy as jnp
from jax import lax

SLABS = 4
BANDS = 2
ROWS = 256
BLK = 128
KB = 2
BSEL = 1
HEADS = 12
HD = 128


def draw_pair(key):
    array_shape = (SLABS, BANDS, ROWS, HEADS * HD)
    first_key, second_key = jax.random.split(key, 2)
    query_field = jnp.clip(jax.random.normal(first_key, array_shape, jnp.float32), -6.0, 6.0)
    key_field = jnp.clip(jax.random.normal(second_key, array_shape, jnp.float32), -6.0, 6.0)
    return (query_field, key_field)


def draw_queries(key, part):
    return draw_pair(jax.random.fold_in(key, 11))[0].astype(jnp.bfloat16)


def draw_keys(key, part):
    return draw_pair(jax.random.fold_in(key, 11))[1].astype(jnp.bfloat16)


def block_orders(key):
    streams = jax.random.split(key, SLABS * BANDS * 2)
    return jax.vmap(lambda stream: jax.random.permutation(stream, KB))(streams)


def draw_adj_mask(key, part):
    orders = block_orders(jax.random.fold_in(key, 23))
    return (orders < KB // 2).astype(jnp.int32).reshape(SLABS, BANDS, 2, KB)


def draw_border_blocks(key, part):
    orders = block_orders(jax.random.fold_in(key, 37))
    return orders[:, :BSEL].astype(jnp.int32).reshape(SLABS, BANDS, 2, BSEL)


def levels(key, extent, cuts, low, high):
    level, own = 1.0, jax.random.fold_in(key, 6)
    for dim, shards_of in cuts:
        heights = jnp.exp(jax.random.uniform(jax.random.fold_in(own, dim), (shards_of,), jnp.float32, low / len(cuts), high / len(cuts)))
        level = level * jnp.repeat(heights, extent[dim] // shards_of).reshape([-1 if axis == dim else 1 for axis in range(len(extent))])
    return level


def normal_values(rng, dims, deviation, most, cuts=(), kind=jnp.bfloat16):
    values = deviation * jax.random.normal(rng, dims, jnp.float32)
    if cuts:
        values = values * levels(rng, dims, cuts, -0.22, 0.18)
    return jnp.clip(values, -most, most).astype(kind)


def setup_inputs(seed: int = 0, part: int = 0) -> dict:
    seeds = jax.random.split(jax.random.key(seed), 6)
    part_keys = jax.random.split(jax.random.fold_in(seeds[5], part), 6)
    queries = draw_queries(jax.random.fold_in(jax.random.fold_in(seeds[5], part), 71), part)
    keys = draw_keys(jax.random.fold_in(jax.random.fold_in(seeds[5], part), 71), part)
    values = normal_values(part_keys[2], (SLABS, BANDS, ROWS, HEADS * HD), 1.0, 6.0, ((0, 4), (1, 2), (3, 2)))
    adj_mask = draw_adj_mask(jax.random.fold_in(jax.random.fold_in(seeds[5], part), 71), part)
    border_blocks = draw_border_blocks(jax.random.fold_in(jax.random.fold_in(seeds[5], part), 71), part)
    return dict(queries=queries, keys=keys, values=values, adj_mask=adj_mask, border_blocks=border_blocks)


masked_score = -1e+30

def attend(query_rows, key_rows, value_rows, bias):
    query_heads = query_rows.reshape(query_rows.shape[0], HEADS, HD).astype(jnp.float32)
    key_heads = key_rows.reshape(key_rows.shape[0], HEADS, HD).astype(jnp.float32)
    value_heads = value_rows.reshape(value_rows.shape[0], HEADS, HD).astype(jnp.float32)
    scores = jnp.einsum('qhd,khd->hqk', query_heads, key_heads) * (1.0 / math.sqrt(HD)) + bias
    maxima = lax.optimization_barrier(jnp.max(scores, axis=2))
    weights = jnp.exp(scores - maxima[:, :, None])
    totals = lax.optimization_barrier(jnp.sum(weights, axis=2))
    rounded = lax.optimization_barrier(weights.astype(jnp.bfloat16)).astype(jnp.float32)
    output = jnp.einsum('hqk,khd->qhd', rounded, value_heads)
    return (maxima, totals, output)

def combine_sources(pieces):
    maxima = jnp.stack([piece[0] for piece in pieces])
    largest = lax.optimization_barrier(jnp.max(maxima, axis=0))
    factors = jnp.exp(maxima - largest)
    numerator = factors[0].T[:, :, None] * pieces[0][2]
    for number in range(1, len(pieces)):
        numerator = numerator + factors[number].T[:, :, None] * pieces[number][2]
    denominator = lax.optimization_barrier(jnp.sum(factors * jnp.stack([piece[1] for piece in pieces]), axis=0))
    return numerator / denominator.T[:, :, None]

def reference(queries, keys, values, adj_mask, border_blocks):

    def one_device(device_index):
        slab_index = device_index // BANDS
        band_index = device_index % BANDS
        prev_slab = jnp.maximum(slab_index - 1, 0)
        next_slab = jnp.minimum(slab_index + 1, SLABS - 1)
        lower_band = jnp.maximum(band_index - 1, 0)
        upper_band = jnp.minimum(band_index + 1, BANDS - 1)
        query_rows = queries[slab_index, band_index]
        own_piece = attend(query_rows, keys[slab_index, band_index], values[slab_index, band_index], jnp.zeros((ROWS,), jnp.float32))
        prev_bias = jnp.where(jnp.repeat(adj_mask[prev_slab, band_index, 0] == 1, BLK) & (slab_index > 0), 0.0, masked_score).astype(jnp.float32)
        prev_piece = attend(query_rows, keys[prev_slab, band_index], values[prev_slab, band_index], prev_bias)
        next_bias = jnp.where(jnp.repeat(adj_mask[next_slab, band_index, 1] == 1, BLK) & (slab_index < SLABS - 1), 0.0, masked_score).astype(jnp.float32)
        next_piece = attend(query_rows, keys[next_slab, band_index], values[next_slab, band_index], next_bias)

        def picked_rows(source, band_from, direction):
            chosen = border_blocks[slab_index, band_from, direction]
            return source[slab_index, band_from].reshape(KB, BLK, HEADS * HD)[chosen].reshape(BSEL * BLK, HEADS * HD)
        rim_rows = BSEL * BLK
        lower_bias = jnp.where(band_index > 0, jnp.zeros((rim_rows,), jnp.float32), jnp.full((rim_rows,), masked_score, jnp.float32))
        upper_bias = jnp.where(band_index < BANDS - 1, jnp.zeros((rim_rows,), jnp.float32), jnp.full((rim_rows,), masked_score, jnp.float32))
        lower_piece = attend(query_rows, picked_rows(keys, lower_band, 1), picked_rows(values, lower_band, 1), lower_bias)
        upper_piece = attend(query_rows, picked_rows(keys, upper_band, 0), picked_rows(values, upper_band, 0), upper_bias)
        merged = combine_sources([own_piece, prev_piece, next_piece, lower_piece, upper_piece])
        return merged.reshape(ROWS, HEADS * HD).astype(jnp.bfloat16)
    results = lax.map(one_device, jnp.arange(SLABS * BANDS, dtype=jnp.int32))
    return results.reshape(SLABS, BANDS, ROWS, HEADS * HD)
```

```python
import functools
import math

import jax
import jax.numpy as jnp
from jax import lax
from jax.experimental import pallas as pl
from jax.experimental.pallas import tpu as pltpu
from jax.sharding import PartitionSpec as P

BLK = 128
HD = 128
MASKED = -1e30
TO_EXP2 = math.log2(math.e) / math.sqrt(HD)


def swaps(axis_sizes):
    return [(axis, phase) for axis, size in axis_sizes for phase in range(min(2, size - 1))]


def swap(value, axis, phase):
    size, spare = lax.axis_size(axis), lax.axis_size("head")
    partner = {}
    for low in range(phase, size - 1, 2):
        partner[low], partner[low + 1] = low + 1, low
    pairs = []
    for here in range(size):
        for head in range(spare):
            if here in partner:
                pairs.append((here * spare + head, partner[here] * spare + head))
            elif spare % 2 == 0:
                pairs.append((here * spare + head, here * spare + (head ^ 1)))
    return lax.ppermute(value, (axis, "head"), pairs)


def pick(plan, adj_mask, border_blocks, keys, values):
    width = keys.shape[1]
    blocks = adj_mask.shape[1]
    counts = [border_blocks.shape[1] if axis == "band" else 1 for axis, _ in plan]

    def kernel(adj_ref, border_ref, key_ref, value_ref, *rest):
        outs, sems = rest[: len(plan)], rest[len(plan)]
        copies = []
        for number, (axis, phase) in enumerate(plan):
            up = lax.rem(lax.axis_index(axis), 2) == phase
            for entry in range(counts[number]):
                if axis == "band":
                    block = border_ref[jnp.where(up, 1, 0), entry]
                else:
                    row = jnp.where(up, 0, 1)
                    block = 0
                    for j in range(1, blocks):
                        block = block + j * adj_ref[row, j]
                rows = pl.ds(pl.multiple_of(block * BLK, BLK), BLK)
                for part, source in enumerate((key_ref, value_ref)):
                    copy = pltpu.make_async_copy(
                        source.at[rows],
                        outs[number].at[pl.ds((part * counts[number] + entry) * BLK, BLK)],
                        sems.at[len(copies)],
                    )
                    copy.start()
                    copies.append(copy)
        for copy in copies:
            copy.wait()

    anywhere = pl.BlockSpec(memory_space=pl.ANY)
    scalar = pl.BlockSpec(memory_space=pltpu.SMEM)
    return pl.pallas_call(
        kernel,
        name="pick",
        out_shape=[pltpu.VMEM((2 * count * BLK, width), keys.dtype) for count in counts],
        in_specs=[scalar, scalar, anywhere, anywhere],
        out_specs=[pl.BlockSpec(memory_space=pltpu.VMEM)] * len(plan),
        scratch_shapes=[pltpu.SemaphoreType.DMA((2 * sum(counts),))],
    )(adj_mask, border_blocks, keys, values)


def score(query, key):
    return lax.dot_general(query, key, (((1,), (1,)), ((), ())), preferred_element_type=jnp.float32) * TO_EXP2


def weigh(weights, value):
    both = jnp.concatenate([value, jnp.ones_like(value)], axis=1)
    return jnp.dot(weights.astype(value.dtype), both, preferred_element_type=jnp.float32)


def own(queries, keys, values):
    rows, width = queries.shape
    heads = width // HD

    def kernel(query_ref, key_ref, value_ref, top_ref, total_ref):
        for head in range(heads):
            cols = slice(head * HD, (head + 1) * HD)
            scores = score(query_ref[:, cols], key_ref[:, cols])
            top = jnp.max(scores, axis=1, keepdims=True)
            total_ref[head] = weigh(jnp.exp2(scores - top), value_ref[:, cols])
            top_ref[head] = jnp.broadcast_to(top, (rows, HD))

    in_vmem = pl.BlockSpec(memory_space=pltpu.VMEM)
    return pl.pallas_call(
        kernel,
        name="own",
        out_shape=[pltpu.VMEM((heads, rows, HD), jnp.float32), pltpu.VMEM((heads, rows, 2 * HD), jnp.float32)],
        in_specs=[in_vmem] * 3,
        out_specs=[in_vmem] * 2,
        cost_estimate=pl.CostEstimate(flops=4 * rows * rows * width, bytes_accessed=6 * rows * width, transcendentals=rows * rows * heads),
    )(queries, keys, values)


def join(queries, swapped, state, axis, phase, last):
    rows, width = queries.shape
    heads = width // HD
    length = swapped.shape[0] // 2
    size = lax.axis_size(axis)

    def kernel(query_ref, swapped_ref, top_ref, total_ref, *outs):
        here = lax.axis_index(axis)
        up = lax.rem(here, 2) == phase
        valid = jnp.where(up, here < size - 1, here > 0)
        bias = jnp.where(valid, 0.0, MASKED).astype(jnp.float32)
        for head in range(heads):
            cols = slice(head * HD, (head + 1) * HD)
            scores = score(query_ref[:, cols], swapped_ref[:length, cols]) + bias
            old_top = top_ref[head]
            top = jnp.maximum(old_top, jnp.max(scores, axis=1, keepdims=True))
            kept = jnp.exp2(old_top - top)
            new = weigh(jnp.exp2(scores - top[:, :1]), swapped_ref[length:, cols])
            total = total_ref[head]
            left = total[:, :HD] * kept + new[:, :HD]
            right = total[:, HD:] * kept + new[:, HD:]
            if last:
                outs[0][:, cols] = (left / right).astype(outs[0].dtype)
            else:
                outs[0][head] = top
                outs[1][head, :, :HD] = left
                outs[1][head, :, HD:] = right

    in_vmem = pl.BlockSpec(memory_space=pltpu.VMEM)
    if last:
        out_shape, out_specs = jax.ShapeDtypeStruct((rows, width), queries.dtype), in_vmem
    else:
        out_shape = [pltpu.VMEM((heads, rows, HD), jnp.float32), pltpu.VMEM((heads, rows, 2 * HD), jnp.float32)]
        out_specs = [in_vmem] * 2
    return pl.pallas_call(
        kernel,
        name="join_" + axis,
        out_shape=out_shape,
        in_specs=[in_vmem] * 4,
        out_specs=out_specs,
        cost_estimate=pl.CostEstimate(flops=4 * rows * length * width, bytes_accessed=6 * rows * width, transcendentals=rows * length * heads),
    )(queries, swapped, *state)


def per_device(queries, keys, values, adj_mask, border_blocks):
    queries, keys, values = queries[0, 0], keys[0, 0], values[0, 0]
    tm, band = lax.axis_size("tm"), lax.axis_size("band")
    plan = swaps((("tm", tm), ("band", band)))
    plan.sort(key=lambda entry: entry[1])
    outgoing = pick(plan, adj_mask[0, 0], border_blocks[0, 0], keys, values)
    incoming = [swap(rows, axis, phase) for rows, (axis, phase) in zip(outgoing, plan)]
    state = own(queries, keys, values)
    for number, (axis, phase) in enumerate(plan):
        state = join(queries, incoming[number], state, axis, phase, number == len(plan) - 1)
    return state[None, None]


def solution(mesh):
    wide = P(("clip", "tm"), "band", None, "head")
    narrow = P(("clip", "tm"), "band", None, None)
    return jax.shard_map(
        per_device, mesh=mesh, in_specs=(wide, wide, wide, narrow, narrow), out_specs=wide, check_vma=False
    )
```

```python
import itertools
import math

import jax
import jax.numpy as jnp
from jax import lax
from jax.experimental import pallas as pl
from jax.experimental.pallas import tpu as pltpu
from jax.sharding import PartitionSpec as P

BLK = 128
HD = 128
MASKED = -1e30
TO_EXP2 = math.log2(math.e) / math.sqrt(HD)
AXES = ("tm", "band", "head")
ROOM = pltpu.CompilerParams(vmem_limit_bytes=16 * 1024 * 1024)
IN_VMEM = pl.BlockSpec(memory_space=pltpu.VMEM)
ANYWHERE = pl.BlockSpec(memory_space=pl.ANY)
ROWS_BY_ROWS = (((1,), (1,)), ((), ()))
COLUMNS_BY_COLUMNS = (((0,), (0,)), ((), ()))


def swap_plan(sizes, border_count):
    steps = [(axis, phase) for axis in ("tm", "band") for phase in range(min(2, sizes[axis] - 1))]
    first, second = ("tm", 0), ("band", 0)
    if first in steps and second in steps and sizes["head"] % 2 == 0 and border_count == 1:
        rest = [step for step in steps if step not in (first, second)]
        return [(first, second)] + [(step, step) for step in rest[:1]] + [(second, first)] + [(step, step) for step in rest[1:]]
    return [(step, step) for step in steps]


def swap(value, choice):
    sizes = {axis: lax.axis_size(axis) for axis in AXES}

    def partner(place):
        axis, phase = choice[place["head"] % 2]
        there = place[axis] + 1 if place[axis] % 2 == phase else place[axis] - 1
        return {**place, axis: there} if 0 <= there < sizes[axis] else None

    def index(place):
        return (place["tm"] * sizes["band"] + place["band"]) * sizes["head"] + place["head"]

    pairs = []
    for numbers in itertools.product(*(range(sizes[axis]) for axis in AXES)):
        place = dict(zip(AXES, numbers))
        other = partner(place)
        if other is None:
            beside = {**place, "head": place["head"] ^ 1}
            if beside["head"] < sizes["head"] and partner(beside) is None:
                other = beside
        if other is not None:
            pairs.append((index(place), index(other)))
    return lax.ppermute(value, AXES, pairs)


def either(choice, function):
    even, odd = (function(*step) for step in choice)
    if choice[0] == choice[1]:
        return even
    return jnp.where(lax.rem(lax.axis_index("head"), 2) == 0, even, odd)


def goes_up(axis, phase):
    return lax.rem(lax.axis_index(axis), 2) == phase


def has_partner(axis, phase):
    here, size = lax.axis_index(axis), lax.axis_size(axis)
    return jnp.where(goes_up(axis, phase), jnp.where(here < size - 1, 1, 0), jnp.where(here > 0, 1, 0))


def pick(plan, adj_mask, border_blocks, keys, values):
    width = keys.shape[1]
    blocks = adj_mask.shape[1]
    counts = [border_blocks.shape[0] if choice[0][0] == "band" else 1 for choice in plan]

    def kernel(adj_hbm, border_hbm, key_hbm, value_hbm, *rest):
        outs, (adj_ref, border_ref, key_ref, value_ref, sems) = rest[: len(plan)], rest[len(plan) :]
        pairs = ((adj_hbm, adj_ref), (border_hbm, border_ref), (key_hbm, key_ref), (value_hbm, value_ref))
        copies = [pltpu.make_async_copy(*pair, sems.at[number]) for number, pair in enumerate(pairs)]
        for copy in copies:
            copy.start()
        for copy in copies:
            copy.wait()
        for out, choice, count in zip(outs, plan, counts):
            for entry in range(count):

                def block(axis, phase):
                    up = goes_up(axis, phase)
                    if axis == "band":
                        return border_ref[entry, jnp.where(up, 1, 0)]
                    row = jnp.where(up, 0, 1)
                    return sum(number * adj_ref[row, number] for number in range(1, blocks))

                rows = pl.ds(pl.multiple_of(either(choice, block) * BLK, BLK), BLK)
                out[pl.ds(entry * BLK, BLK)] = key_ref[rows]
                out[pl.ds((count + entry) * BLK, BLK)] = value_ref[rows]

    arrays = (adj_mask, border_blocks, keys, values)
    return pl.pallas_call(
        kernel,
        name="pick",
        compiler_params=ROOM,
        out_shape=[pltpu.VMEM((2 * count * BLK, width), keys.dtype) for count in counts],
        in_specs=[ANYWHERE] * 4,
        out_specs=[IN_VMEM] * len(plan),
        scratch_shapes=[pltpu.SMEM(array.shape, array.dtype) for array in arrays[:2]]
        + [pltpu.VMEM(array.shape, array.dtype) for array in arrays[2:]]
        + [pltpu.SemaphoreType.DMA((4,))],
    )(*(pltpu.with_memory_space_constraint(array, pltpu.HBM) for array in arrays))


def score(key, query):
    return lax.dot_general(key, query, ROWS_BY_ROWS, preferred_element_type=jnp.float32) * TO_EXP2


def weigh(value, weights):
    return lax.dot_general(value, weights, COLUMNS_BY_COLUMNS, preferred_element_type=jnp.float32)


def state_shapes(heads, rows):
    return [pltpu.VMEM((heads, height, rows), jnp.float32) for height in (1, 1, HD)]


def cost(rows, keys, width):
    return pl.CostEstimate(
        flops=4 * rows * keys * width, bytes_accessed=2 * (rows + 2 * keys) * width, transcendentals=rows * keys * (width // HD)
    )


def own(queries, keys, values):
    rows, width = queries.shape
    heads = width // HD

    def kernel(query_ref, key_ref, value_ref, top_ref, total_ref, part_ref):
        for head in range(heads):
            cols = slice(head * HD, (head + 1) * HD)
            scores = score(key_ref[:, cols], query_ref[:, cols])
            top = jnp.max(scores, axis=0, keepdims=True)
            weights = jnp.exp2(scores - top)
            top_ref[head] = top
            total_ref[head] = jnp.sum(weights, axis=0, keepdims=True)
            part_ref[head] = weigh(value_ref[:, cols], weights.astype(value_ref.dtype))

    return pl.pallas_call(
        kernel,
        name="own",
        compiler_params=ROOM,
        out_shape=state_shapes(heads, rows),
        in_specs=[IN_VMEM] * 3,
        out_specs=[IN_VMEM] * 3,
        cost_estimate=cost(rows, keys.shape[0], width),
    )(queries, keys, values)


def join(queries, sources, choices, state, last):
    rows, width = queries.shape
    heads = width // HD
    lengths = [source.shape[0] // 2 for source in sources]

    def kernel(query_ref, *rest):
        source_refs, (top_ref, total_ref, part_ref), outs = rest[: len(sources)], rest[len(sources) :][:3], rest[len(sources) + 3 :]
        biases = [jnp.where(either(choice, has_partner) == 1, 0.0, MASKED).astype(jnp.float32) for choice in choices]
        columns = [slice(head * HD, (head + 1) * HD) for head in range(heads)]
        scores = [
            [score(ref[:length, cols], query_ref[:, cols]) for ref, length in zip(source_refs, lengths)] for cols in columns
        ]
        softened = []
        for head in range(heads):
            before = top_ref[head]
            top = before
            for part, bias in zip(scores[head], biases):
                top = jnp.maximum(top, jnp.max(part, axis=0, keepdims=True) + bias)
            weights = [jnp.exp2(part - (top - bias)) for part, bias in zip(scores[head], biases)]
            kept = jnp.exp2(before - top)
            total = total_ref[head] * kept
            for part in weights:
                total = total + jnp.sum(part, axis=0, keepdims=True)
            softened.append((top, kept, total, jnp.concatenate([part.astype(query_ref.dtype) for part in weights])))
        parts = [
            weigh(jnp.concatenate([ref[length:, cols] for ref, length in zip(source_refs, lengths)]), softened[head][3])
            for head, cols in enumerate(columns)
        ]
        copies = []
        for head, cols in enumerate(columns):
            top, kept, total, _ = softened[head]
            part = part_ref[head] * kept + parts[head]
            if last:
                out_hbm, out_ref, sems = outs
                out_ref[head] = (part * (1.0 / total)).astype(out_ref.dtype).T
                copies.append(pltpu.make_async_copy(out_ref.at[head], out_hbm.at[:, cols], sems.at[head]))
                copies[-1].start()
            else:
                outs[0][head], outs[1][head], outs[2][head] = top, total, part
        for copy in copies:
            copy.wait()

    operands = [pltpu.with_memory_space_constraint(array, pltpu.VMEM) for array in (queries, *sources, *state)]
    return pl.pallas_call(
        kernel,
        name="finish" if last else "join",
        compiler_params=ROOM,
        out_shape=pltpu.HBM((rows, width), queries.dtype) if last else state_shapes(heads, rows),
        in_specs=[IN_VMEM] * len(operands),
        out_specs=ANYWHERE if last else [IN_VMEM] * 3,
        scratch_shapes=[pltpu.VMEM((heads, rows, HD), queries.dtype), pltpu.SemaphoreType.DMA((heads,))] if last else [],
        cost_estimate=cost(rows, sum(lengths), width),
    )(*operands)


def per_device(queries, keys, values, adj_mask, border_blocks):
    queries, keys, values = queries[0, 0], keys[0, 0], values[0, 0]
    border_blocks = border_blocks[0, 0].T
    plan = swap_plan({axis: lax.axis_size(axis) for axis in AXES}, border_blocks.shape[0])
    outgoing = pick(plan, adj_mask[0, 0], border_blocks, keys, values)
    incoming = [swap(rows, choice) for rows, choice in zip(outgoing, plan)]
    state = own(queries, keys, values)
    cut = max(0, len(plan) - 2)
    for number in range(cut):
        state = join(queries, incoming[number : number + 1], plan[number : number + 1], state, False)
    return join(queries, incoming[cut:], plan[cut:], state, True)[None, None]


def solution(mesh):
    wide = P(("clip", "tm"), "band", None, "head")
    narrow = P(("clip", "tm"), "band", None, None)
    return jax.shard_map(
        per_device, mesh=mesh, in_specs=(wide, wide, wide, narrow, narrow), out_specs=wide, check_vma=False
    )
```

```python
import itertools
import math

import jax
import jax.numpy as jnp
from jax import lax
from jax.experimental import pallas as pl
from jax.experimental.pallas import tpu as pltpu
from jax.sharding import PartitionSpec as P

BLK = 128
HD = 128
MASKED = -1e30
TO_EXP2 = math.log2(math.e) / math.sqrt(HD)
AXES = ("tm", "band", "head")
ROOM = pltpu.CompilerParams(vmem_limit_bytes=16 * 1024 * 1024)
IN_VMEM = pl.BlockSpec(memory_space=pltpu.VMEM)
ANYWHERE = pl.BlockSpec(memory_space=pl.ANY)
ROWS_BY_ROWS = (((1,), (1,)), ((), ()))
COLUMNS_BY_COLUMNS = (((0,), (0,)), ((), ()))


def swap_plan(sizes, border_count):
    steps = [(axis, phase) for axis in ("tm", "band") for phase in range(min(2, sizes[axis] - 1))]
    first, second = ("tm", 0), ("band", 0)
    if first in steps and second in steps and sizes["head"] % 2 == 0 and border_count == 1:
        rest = [step for step in steps if step not in (first, second)]
        return [(first, second)] + [(step, step) for step in rest[:1]] + [(second, first)] + [(step, step) for step in rest[1:]]
    return [(step, step) for step in steps]


def swap(value, choice):
    sizes = {axis: lax.axis_size(axis) for axis in AXES}

    def partner(place):
        axis, phase = choice[place["head"] % 2]
        there = place[axis] + 1 if place[axis] % 2 == phase else place[axis] - 1
        return {**place, axis: there} if 0 <= there < sizes[axis] else None

    def index(place):
        return (place["tm"] * sizes["band"] + place["band"]) * sizes["head"] + place["head"]

    pairs = []
    for numbers in itertools.product(*(range(sizes[axis]) for axis in AXES)):
        place = dict(zip(AXES, numbers))
        other = partner(place)
        if other is None:
            beside = {**place, "head": place["head"] ^ 1}
            if beside["head"] < sizes["head"] and partner(beside) is None:
                other = beside
        if other is not None:
            pairs.append((index(place), index(other)))
    return lax.ppermute(value, AXES, pairs)


def either(choice, function):
    even, odd = (function(*step) for step in choice)
    if choice[0] == choice[1]:
        return even
    return jnp.where(lax.rem(lax.axis_index("head"), 2) == 0, even, odd)


def goes_up(axis, phase):
    return lax.rem(lax.axis_index(axis), 2) == phase


def has_partner(axis, phase):
    here, size = lax.axis_index(axis), lax.axis_size(axis)
    return jnp.where(goes_up(axis, phase), jnp.where(here < size - 1, 1, 0), jnp.where(here > 0, 1, 0))


def pick(plan, adj_mask, border_blocks, keys, values):
    width = keys.shape[1]
    blocks = adj_mask.shape[1]
    counts = [border_blocks.shape[0] if choice[0][0] == "band" else 1 for choice in plan]

    def kernel(adj_hbm, border_hbm, key_hbm, value_hbm, *rest):
        outs, (key_ref, value_ref, adj_ref, border_ref, sems) = rest[: len(plan)], rest[len(plan) :]
        pairs = ((adj_hbm, adj_ref), (border_hbm, border_ref), (key_hbm, key_ref), (value_hbm, value_ref))
        copies = [pltpu.make_async_copy(*pair, sems.at[number]) for number, pair in enumerate(pairs)]
        for copy in copies:
            copy.start()
        for copy in copies[:2]:
            copy.wait()
        chosen = []
        for out, choice, count in zip(outs, plan, counts):
            for entry in range(count):

                def block(axis, phase):
                    up = goes_up(axis, phase)
                    if axis == "band":
                        return border_ref[entry, jnp.where(up, 1, 0)]
                    row = jnp.where(up, 0, 1)
                    return sum(number * adj_ref[row, number] for number in range(1, blocks))

                rows = pl.ds(pl.multiple_of(either(choice, block) * BLK, BLK), BLK)
                chosen.append((out, rows, entry * BLK, (count + entry) * BLK))
        copies[2].wait()
        for out, rows, place, _ in chosen:
            out[pl.ds(place, BLK)] = key_ref[rows]
        copies[3].wait()
        for out, rows, _, place in chosen:
            out[pl.ds(place, BLK)] = value_ref[rows]

    arrays = (adj_mask, border_blocks, keys, values)
    return pl.pallas_call(
        kernel,
        name="pick",
        compiler_params=ROOM,
        out_shape=[pltpu.VMEM((2 * count * BLK, width), keys.dtype) for count in counts]
        + [pltpu.VMEM(array.shape, array.dtype) for array in arrays[2:]],
        in_specs=[ANYWHERE] * 4,
        out_specs=[IN_VMEM] * (len(plan) + 2),
        scratch_shapes=[pltpu.SMEM(array.shape, array.dtype) for array in arrays[:2]] + [pltpu.SemaphoreType.DMA((4,))],
    )(*(pltpu.with_memory_space_constraint(array, pltpu.HBM) for array in arrays))


def score(key, query):
    return lax.dot_general(key, query, ROWS_BY_ROWS, preferred_element_type=jnp.float32) * TO_EXP2


def weigh(value, weights):
    return lax.dot_general(value, weights, COLUMNS_BY_COLUMNS, preferred_element_type=jnp.float32)


def state_shapes(heads, rows):
    return [pltpu.VMEM((heads, height, rows), jnp.float32) for height in (1, 1, HD)]


def cost(rows, keys, width):
    return pl.CostEstimate(
        flops=4 * rows * keys * width, bytes_accessed=2 * (rows + 2 * keys) * width, transcendentals=rows * keys * (width // HD)
    )


def own(queries, keys, values):
    rows, width = queries.shape
    heads = width // HD

    def kernel(query_ref, key_ref, value_ref, top_ref, total_ref, part_ref):
        columns = [slice(head * HD, (head + 1) * HD) for head in range(heads)]
        scores = [score(key_ref[:, cols], query_ref[:, cols]) for cols in columns]
        rounded = []
        for head in range(heads):
            top = jnp.max(scores[head], axis=0, keepdims=True)
            weights = jnp.exp2(scores[head] - top)
            top_ref[head] = top
            total_ref[head] = jnp.sum(weights, axis=0, keepdims=True)
            rounded.append(weights.astype(value_ref.dtype))
        for head, cols in enumerate(columns):
            part_ref[head] = weigh(value_ref[:, cols], rounded[head])

    return pl.pallas_call(
        kernel,
        name="own",
        compiler_params=ROOM,
        out_shape=state_shapes(heads, rows),
        in_specs=[IN_VMEM] * 3,
        out_specs=[IN_VMEM] * 3,

    )(*(pltpu.with_memory_space_constraint(array, pltpu.VMEM) for array in (queries, keys, values)))


def join(queries, sources, choices, state, last):
    rows, width = queries.shape
    heads = width // HD
    lengths = [source.shape[0] // 2 for source in sources]

    def kernel(query_ref, *rest):
        source_refs, (top_ref, total_ref, part_ref), outs = rest[: len(sources)], rest[len(sources) :][:3], rest[len(sources) + 3 :]
        biases = [jnp.where(either(choice, has_partner) == 1, 0.0, MASKED).astype(jnp.float32) for choice in choices]
        columns = [slice(head * HD, (head + 1) * HD) for head in range(heads)]
        scores = [
            [score(ref[:length, cols], query_ref[:, cols]) for ref, length in zip(source_refs, lengths)] for cols in columns
        ]
        softened = []
        for head in range(heads):
            before = top_ref[head]
            top = before
            for part, bias in zip(scores[head], biases):
                top = jnp.maximum(top, jnp.max(part, axis=0, keepdims=True) + bias)
            weights = [jnp.exp2(part - (top - bias)) for part, bias in zip(scores[head], biases)]
            kept = jnp.exp2(before - top)
            total = total_ref[head] * kept
            for part in weights:
                total = total + jnp.sum(part, axis=0, keepdims=True)
            softened.append((top, kept, total, jnp.concatenate([part.astype(query_ref.dtype) for part in weights])))
        parts = [
            weigh(jnp.concatenate([ref[length:, cols] for ref, length in zip(source_refs, lengths)]), softened[head][3])
            for head, cols in enumerate(columns)
        ]
        copies = []
        for head, cols in enumerate(columns):
            top, kept, total, _ = softened[head]
            part = part_ref[head] * kept + parts[head]
            if last:
                out_hbm, out_ref, sems = outs
                out_ref[head] = (part * (1.0 / total)).astype(out_ref.dtype).T
                copies.append(pltpu.make_async_copy(out_ref.at[head], out_hbm.at[:, cols], sems.at[head]))
                copies[-1].start()
            else:
                outs[0][head], outs[1][head], outs[2][head] = top, total, part
        for copy in copies:
            copy.wait()

    operands = [pltpu.with_memory_space_constraint(array, pltpu.VMEM) for array in (queries, *sources, *state)]
    return pl.pallas_call(
        kernel,
        name="finish" if last else "join",
        compiler_params=ROOM,
        out_shape=pltpu.HBM((rows, width), queries.dtype) if last else state_shapes(heads, rows),
        in_specs=[IN_VMEM] * len(operands),
        out_specs=ANYWHERE if last else [IN_VMEM] * 3,
        scratch_shapes=[pltpu.VMEM((heads, rows, HD), queries.dtype), pltpu.SemaphoreType.DMA((heads,))] if last else [],
        cost_estimate=cost(rows, sum(lengths), width),
    )(*operands)


def per_device(queries, keys, values, adj_mask, border_blocks):
    queries, keys, values = queries[0, 0], keys[0, 0], values[0, 0]
    border_blocks = border_blocks[0, 0].T
    plan = swap_plan({axis: lax.axis_size(axis) for axis in AXES}, border_blocks.shape[0])
    *outgoing, keys, values = pick(plan, adj_mask[0, 0], border_blocks, keys, values)
    state = own(queries, keys, values)
    for number in range(2, len(plan)):
        outgoing[number], state = lax.optimization_barrier((outgoing[number], state))
    incoming = [swap(rows, choice) for rows, choice in zip(outgoing, plan)]
    cut = max(0, len(plan) - 2)
    for number in range(cut):
        state = join(queries, incoming[number : number + 1], plan[number : number + 1], state, False)
    return join(queries, incoming[cut:], plan[cut:], state, True)[None, None]


def solution(mesh):
    wide = P(("clip", "tm"), "band", None, "head")
    narrow = P(("clip", "tm"), "band", None, None)
    return jax.shard_map(
        per_device, mesh=mesh, in_specs=(wide, wide, wide, narrow, narrow), out_specs=wide, check_vma=False
    )
```

```python
import functools
import itertools
import math

import jax
import jax.numpy as jnp
from jax import lax
from jax.experimental import pallas as pl
from jax.experimental.pallas import tpu as pltpu
from jax.sharding import PartitionSpec as P

BLK = 128
HD = 128
MASKED = -1e30
SAFE_TOTAL = 2.0**90
TO_EXP2 = math.log2(math.e) / math.sqrt(HD)
AXES = ("tm", "band", "head")
ROOM = pltpu.CompilerParams(vmem_limit_bytes=16 * 1024 * 1024)
IN_VMEM = pl.BlockSpec(memory_space=pltpu.VMEM)
ANYWHERE = pl.BlockSpec(memory_space=pl.ANY)
ROWS_BY_ROWS = (((1,), (1,)), ((), ()))
COLUMNS_BY_COLUMNS = (((0,), (0,)), ((), ()))


def swap_plan(sizes, border_count):
    steps = [(axis, phase) for axis in ("tm", "band") for phase in range(min(2, sizes[axis] - 1))]
    first, second = ("tm", 0), ("band", 0)
    if first in steps and second in steps and sizes["head"] % 2 == 0 and border_count == 1:
        rest = [step for step in steps if step not in (first, second)]
        return [(first, second)] + [(step, step) for step in rest[:1]] + [(second, first)] + [(step, step) for step in rest[1:]]
    return [(step, step) for step in steps]


def swap(value, choice):
    sizes = {axis: lax.axis_size(axis) for axis in AXES}

    def partner(place):
        axis, phase = choice[place["head"] % 2]
        there = place[axis] + 1 if place[axis] % 2 == phase else place[axis] - 1
        return {**place, axis: there} if 0 <= there < sizes[axis] else None

    def index(place):
        return (place["tm"] * sizes["band"] + place["band"]) * sizes["head"] + place["head"]

    pairs = []
    for numbers in itertools.product(*(range(sizes[axis]) for axis in AXES)):
        place = dict(zip(AXES, numbers))
        other = partner(place)
        if other is None:
            beside = {**place, "head": place["head"] ^ 1}
            if beside["head"] < sizes["head"] and partner(beside) is None:
                other = beside
        if other is not None:
            pairs.append((index(place), index(other)))
    return lax.ppermute(value, AXES, pairs)


def either(choice, function):
    even, odd = (function(*step) for step in choice)
    if choice[0] == choice[1]:
        return even
    return jnp.where(lax.rem(lax.axis_index("head"), 2) == 0, even, odd)


def goes_up(axis, phase):
    return lax.rem(lax.axis_index(axis), 2) == phase


def has_partner(axis, phase):
    here, size = lax.axis_index(axis), lax.axis_size(axis)
    return jnp.where(goes_up(axis, phase), jnp.where(here < size - 1, 1, 0), jnp.where(here > 0, 1, 0))


def pick(plan, adj_mask, border_blocks, keys, values):
    width = keys.shape[1]
    blocks = adj_mask.shape[1]
    counts = [border_blocks.shape[0] if choice[0][0] == "band" else 1 for choice in plan]

    def kernel(adj_hbm, border_hbm, key_hbm, value_hbm, *rest):
        outs, (key_ref, value_ref, adj_ref, border_ref, sems) = rest[: len(plan)], rest[len(plan) :]
        pairs = ((adj_hbm, adj_ref), (border_hbm, border_ref), (key_hbm, key_ref), (value_hbm, value_ref))
        copies = [pltpu.make_async_copy(*pair, sems.at[number]) for number, pair in enumerate(pairs)]
        for copy in copies:
            copy.start()
        for copy in copies[:2]:
            copy.wait()
        chosen = []
        for out, choice, count in zip(outs, plan, counts):
            for entry in range(count):

                def block(axis, phase):
                    up = goes_up(axis, phase)
                    if axis == "band":
                        return border_ref[entry, jnp.where(up, 1, 0)]
                    row = jnp.where(up, 0, 1)
                    return sum(number * adj_ref[row, number] for number in range(1, blocks))

                rows = pl.ds(pl.multiple_of(either(choice, block) * BLK, BLK), BLK)
                chosen.append((out, rows, entry * BLK, (count + entry) * BLK))
        copies[2].wait()
        for out, rows, place, _ in chosen:
            out[pl.ds(place, BLK)] = key_ref[rows]
        copies[3].wait()
        for out, rows, _, place in chosen:
            out[pl.ds(place, BLK)] = value_ref[rows]

    arrays = (adj_mask, border_blocks, keys, values)
    return pl.pallas_call(
        kernel,
        name="pick",
        compiler_params=ROOM,
        out_shape=[pltpu.VMEM((2 * count * BLK, width), keys.dtype) for count in counts]
        + [pltpu.VMEM(array.shape, array.dtype) for array in arrays[2:]],
        in_specs=[ANYWHERE] * 4,
        out_specs=[IN_VMEM] * (len(plan) + 2),
        scratch_shapes=[pltpu.SMEM(array.shape, array.dtype) for array in arrays[:2]] + [pltpu.SemaphoreType.DMA((4,))],
    )(*(pltpu.with_memory_space_constraint(array, pltpu.HBM) for array in arrays))


def score(key, query):
    return lax.dot_general(key, query, ROWS_BY_ROWS, preferred_element_type=jnp.float32) * TO_EXP2


def weigh(value, weights):
    return lax.dot_general(value, weights, COLUMNS_BY_COLUMNS, preferred_element_type=jnp.float32)


def state_shapes(heads, rows):
    return [pltpu.VMEM((heads, height, rows), jnp.float32) for height in (1, 1, HD)]


def cost(rows, keys, width):
    return pl.CostEstimate(
        flops=4 * rows * keys * width, bytes_accessed=2 * (rows + 2 * keys) * width, transcendentals=rows * keys * (width // HD)
    )


def own(queries, keys, values):
    rows, width = queries.shape
    heads = width // HD

    def kernel(query_ref, key_ref, value_ref, top_ref, total_ref, part_ref):
        columns = [slice(head * HD, (head + 1) * HD) for head in range(heads)]
        scores = [score(key_ref[:, cols], query_ref[:, cols]) for cols in columns]
        rounded = []
        for head in range(heads):
            top = jnp.max(scores[head], axis=0, keepdims=True)
            weights = jnp.exp2(scores[head] - top)
            top_ref[head] = top
            total_ref[head] = jnp.sum(weights, axis=0, keepdims=True)
            rounded.append(weights.astype(value_ref.dtype))
        for head, cols in enumerate(columns):
            part_ref[head] = weigh(value_ref[:, cols], rounded[head])

    return pl.pallas_call(
        kernel,
        name="own",
        compiler_params=ROOM,
        out_shape=state_shapes(heads, rows),
        in_specs=[IN_VMEM] * 3,
        out_specs=[IN_VMEM] * 3,

    )(*(pltpu.with_memory_space_constraint(array, pltpu.VMEM) for array in (queries, keys, values)))


def split(refs, lengths, cols, values):
    return [ref[length:, cols] if values else ref[:length, cols] for ref, length in zip(refs, lengths)]


def join(queries, source, choice, state):
    rows, width = queries.shape
    heads = width // HD
    length = source.shape[0] // 2

    def kernel(query_ref, source_ref, top_ref, total_ref, part_ref, new_top_ref, new_total_ref, new_part_ref):
        bias = jnp.where(either(choice, has_partner) == 1, 0.0, MASKED).astype(jnp.float32)
        columns = [slice(head * HD, (head + 1) * HD) for head in range(heads)]
        scores = [score(source_ref[:length, cols], query_ref[:, cols]) for cols in columns]
        rounded, kept = [], []
        for head in range(heads):
            top = jnp.maximum(top_ref[head], jnp.max(scores[head], axis=0, keepdims=True) + bias)
            weights = jnp.exp2(scores[head] - (top - bias))
            kept.append(jnp.exp2(top_ref[head] - top))
            new_top_ref[head] = top
            new_total_ref[head] = total_ref[head] * kept[head] + jnp.sum(weights, axis=0, keepdims=True)
            rounded.append(weights.astype(query_ref.dtype))
        for head, cols in enumerate(columns):
            new_part_ref[head] = part_ref[head] * kept[head] + weigh(source_ref[length:, cols], rounded[head])

    operands = [pltpu.with_memory_space_constraint(array, pltpu.VMEM) for array in (queries, source, *state)]
    return pl.pallas_call(
        kernel,
        name="join",
        compiler_params=ROOM,
        out_shape=state_shapes(heads, rows),
        in_specs=[IN_VMEM] * len(operands),
        out_specs=[IN_VMEM] * 3,
        cost_estimate=cost(rows, length, width),
    )(*operands)


def finish(queries, sources, choices, state):
    rows, width = queries.shape
    heads = width // HD
    count = len(sources)
    lengths = [source.shape[0] // 2 for source in sources]

    def kernel(query_ref, *rest):
        source_refs, (top_ref, total_ref, part_ref, out_hbm, out_ref, sems) = rest[:count], rest[count:]
        biases = [jnp.where(either(choice, has_partner) == 1, 0.0, MASKED).astype(jnp.float32) for choice in choices]
        columns = [slice(head * HD, (head + 1) * HD) for head in range(heads)]

        def run(true_maximum):
            scores = [[score(key, query_ref[:, cols]) for key in split(source_refs, lengths, cols, False)] for cols in columns]
            rounded, totals, kept = [], [], []
            for head in range(heads):
                top = before = top_ref[head]
                if true_maximum:
                    for part, bias in zip(scores[head], biases):
                        top = jnp.maximum(top, jnp.max(part, axis=0, keepdims=True) + bias)
                weights = [jnp.exp2(part - (top - bias)) for part, bias in zip(scores[head], biases)]
                kept.append(jnp.exp2(before - top) if true_maximum else 1.0)
                totals.append(total_ref[head] * kept[head] + sum(jnp.sum(part, axis=0, keepdims=True) for part in weights))
                rounded.append(jnp.concatenate([part.astype(query_ref.dtype) for part in weights]))
            parts = [
                weigh(jnp.concatenate(split(source_refs, lengths, cols, True)), rounded[head])
                for head, cols in enumerate(columns)
            ]
            copies = []
            for head, cols in enumerate(columns):
                part = part_ref[head] * kept[head] + parts[head]
                out_ref[head] = (part * (1.0 / totals[head])).astype(out_ref.dtype).T
                copies.append(pltpu.make_async_copy(out_ref.at[head], out_hbm.at[:, cols], sems.at[head]))
                copies[-1].start()
            small = functools.reduce(jnp.logical_and, [total < SAFE_TOTAL for total in totals])
            far = jnp.max(jnp.where(small, 0, 1))
            for copy in copies:
                copy.wait()
            return far

        far = run(False)

        @pl.when(far > 0)
        def _():
            run(True)

    operands = [pltpu.with_memory_space_constraint(array, pltpu.VMEM) for array in (queries, *sources, *state)]
    return pl.pallas_call(
        kernel,
        name="finish",
        compiler_params=ROOM,
        out_shape=pltpu.HBM((rows, width), queries.dtype),
        in_specs=[IN_VMEM] * len(operands),
        out_specs=ANYWHERE,
        scratch_shapes=[pltpu.VMEM((heads, rows, HD), queries.dtype), pltpu.SemaphoreType.DMA((heads,))],
        cost_estimate=cost(rows, sum(lengths), width),
    )(*operands)


def per_device(queries, keys, values, adj_mask, border_blocks):
    queries, keys, values = queries[0, 0], keys[0, 0], values[0, 0]
    border_blocks = border_blocks[0, 0].T
    plan = swap_plan({axis: lax.axis_size(axis) for axis in AXES}, border_blocks.shape[0])
    *outgoing, keys, values = pick(plan, adj_mask[0, 0], border_blocks, keys, values)
    state = own(queries, keys, values)
    for number in range(2, len(plan)):
        outgoing[number], state = lax.optimization_barrier((outgoing[number], state))
    incoming = [swap(rows, choice) for rows, choice in zip(outgoing, plan)]
    cut = max(0, len(plan) - 2)
    for number in range(cut):
        state = join(queries, incoming[number], plan[number], state)
    return finish(queries, incoming[cut:], plan[cut:], state)[None, None]


def solution(mesh):
    wide = P(("clip", "tm"), "band", None, "head")
    narrow = P(("clip", "tm"), "band", None, None)
    return jax.shard_map(
        per_device, mesh=mesh, in_specs=(wide, wide, wide, narrow, narrow), out_specs=wide, check_vma=False
    )
```

```python
import functools
import itertools
import math

import jax
import jax.numpy as jnp
from jax import lax
from jax.experimental import pallas as pl
from jax.experimental.pallas import tpu as pltpu
from jax.sharding import PartitionSpec as P

BLK = 128
HD = 128
MASKED = -1e30
SAFE_TOTAL = 2.0**90
LAST_SHARE = 3
LAST_SOURCES = 3
TO_EXP2 = math.log2(math.e) / math.sqrt(HD)
AXES = ("tm", "band", "head")
ROOM = pltpu.CompilerParams(vmem_limit_bytes=16 * 1024 * 1024)
IN_VMEM = pl.BlockSpec(memory_space=pltpu.VMEM)
ANYWHERE = pl.BlockSpec(memory_space=pl.ANY)
ROWS_BY_ROWS = (((1,), (1,)), ((), ()))
COLUMNS_BY_COLUMNS = (((0,), (0,)), ((), ()))


def swap_plan(sizes, border_count):
    steps = [(axis, phase) for axis in ("tm", "band") for phase in range(min(2, sizes[axis] - 1))]
    first, second = ("tm", 0), ("band", 0)
    if first in steps and second in steps and sizes["head"] % 2 == 0 and border_count == 1:
        rest = [step for step in steps if step not in (first, second)]
        return [(first, second)] + [(step, step) for step in rest[:1]] + [(second, first)] + [(step, step) for step in rest[1:]]
    return [(step, step) for step in steps]


def swap(value, choice):
    sizes = {axis: lax.axis_size(axis) for axis in AXES}

    def partner(place):
        axis, phase = choice[place["head"] % 2]
        there = place[axis] + 1 if place[axis] % 2 == phase else place[axis] - 1
        return {**place, axis: there} if 0 <= there < sizes[axis] else None

    def index(place):
        return (place["tm"] * sizes["band"] + place["band"]) * sizes["head"] + place["head"]

    pairs = []
    for numbers in itertools.product(*(range(sizes[axis]) for axis in AXES)):
        place = dict(zip(AXES, numbers))
        other = partner(place)
        if other is None:
            beside = {**place, "head": place["head"] ^ 1}
            if beside["head"] < sizes["head"] and partner(beside) is None:
                other = beside
        if other is not None:
            pairs.append((index(place), index(other)))
    return lax.ppermute(value, AXES, pairs)


def either(choice, function):
    even, odd = (function(*step) for step in choice)
    if choice[0] == choice[1]:
        return even
    return jnp.where(lax.rem(lax.axis_index("head"), 2) == 0, even, odd)


def goes_up(axis, phase):
    return lax.rem(lax.axis_index(axis), 2) == phase


def has_partner(axis, phase):
    here, size = lax.axis_index(axis), lax.axis_size(axis)
    return jnp.where(goes_up(axis, phase), jnp.where(here < size - 1, 1, 0), jnp.where(here > 0, 1, 0))


def pick(plan, pieces, adj_mask, border_blocks, keys, values):
    blocks = adj_mask.shape[1]
    counts = [border_blocks.shape[0] if choice[0][0] == "band" else 1 for choice in plan]
    shapes = [(2 * count * BLK, piece.stop - piece.start) for count, cuts in zip(counts, pieces) for piece in cuts]

    def kernel(adj_hbm, border_hbm, key_hbm, value_hbm, *rest):
        outs, (key_ref, value_ref, adj_ref, border_ref, sems) = iter(rest[: len(shapes)]), rest[len(shapes) :]
        pairs = ((adj_hbm, adj_ref), (border_hbm, border_ref), (key_hbm, key_ref), (value_hbm, value_ref))
        copies = [pltpu.make_async_copy(*pair, sems.at[number]) for number, pair in enumerate(pairs)]
        for copy in copies:
            copy.start()
        for copy in copies[:2]:
            copy.wait()
        chosen = []
        for choice, count, cuts in zip(plan, counts, pieces):
            cut_outs = [(piece, next(outs)) for piece in cuts]
            for entry in range(count):

                def block(axis, phase):
                    up = goes_up(axis, phase)
                    if axis == "band":
                        return border_ref[entry, jnp.where(up, 1, 0)]
                    row = jnp.where(up, 0, 1)
                    return sum(number * adj_ref[row, number] for number in range(1, blocks))

                rows = pl.ds(pl.multiple_of(either(choice, block) * BLK, BLK), BLK)
                chosen += [(out, piece, rows, entry * BLK, (count + entry) * BLK) for piece, out in cut_outs]
        copies[2].wait()
        for out, piece, rows, place, _ in chosen:
            out[pl.ds(place, BLK)] = key_ref[rows, piece]
        copies[3].wait()
        for out, piece, rows, _, place in chosen:
            out[pl.ds(place, BLK)] = value_ref[rows, piece]

    arrays = (adj_mask, border_blocks, keys, values)
    *outgoing, keys, values = pl.pallas_call(
        kernel,
        name="pick",
        compiler_params=ROOM,
        out_shape=[pltpu.VMEM(shape, keys.dtype) for shape in shapes]
        + [pltpu.VMEM(array.shape, array.dtype) for array in arrays[2:]],
        in_specs=[ANYWHERE] * 4,
        out_specs=[IN_VMEM] * (len(shapes) + 2),
        scratch_shapes=[pltpu.SMEM(array.shape, array.dtype) for array in arrays[:2]] + [pltpu.SemaphoreType.DMA((4,))],
    )(*(pltpu.with_memory_space_constraint(array, pltpu.HBM) for array in arrays))
    outgoing = iter(outgoing)
    return [[next(outgoing) for _ in cuts] for cuts in pieces], keys, values


def score(key, query):
    return lax.dot_general(key, query, ROWS_BY_ROWS, preferred_element_type=jnp.float32) * TO_EXP2


def weigh(value, weights):
    return lax.dot_general(value, weights, COLUMNS_BY_COLUMNS, preferred_element_type=jnp.float32)


def state_shapes(heads, rows):
    return [pltpu.VMEM((heads, height, rows), jnp.float32) for height in (1, 1, HD)]


def cost(rows, keys, width):
    return pl.CostEstimate(
        flops=4 * rows * keys * width, bytes_accessed=2 * (rows + 2 * keys) * width, transcendentals=rows * keys * (width // HD)
    )


def own(queries, keys, values):
    rows, width = queries.shape
    heads = width // HD

    def kernel(query_ref, key_ref, value_ref, top_ref, total_ref, part_ref):
        columns = [slice(head * HD, (head + 1) * HD) for head in range(heads)]
        scores = [score(key_ref[:, cols], query_ref[:, cols]) for cols in columns]
        rounded = []
        for head in range(heads):
            top = jnp.max(scores[head], axis=0, keepdims=True)
            weights = jnp.exp2(scores[head] - top)
            top_ref[head] = top
            total_ref[head] = jnp.sum(weights, axis=0, keepdims=True)
            rounded.append(weights.astype(value_ref.dtype))
        for head, cols in enumerate(columns):
            part_ref[head] = weigh(value_ref[:, cols], rounded[head])

    return pl.pallas_call(
        kernel,
        name="own",
        compiler_params=ROOM,
        out_shape=state_shapes(heads, rows),
        in_specs=[IN_VMEM] * 3,
        out_specs=[IN_VMEM] * 3,

    )(*(pltpu.with_memory_space_constraint(array, pltpu.VMEM) for array in (queries, keys, values)))


def join(queries, source, choice, state):
    rows, width = queries.shape
    heads = width // HD
    length = source.shape[0] // 2

    def kernel(query_ref, source_ref, top_ref, total_ref, part_ref, new_top_ref, new_total_ref, new_part_ref):
        bias = jnp.where(either(choice, has_partner) == 1, 0.0, MASKED).astype(jnp.float32)
        columns = [slice(head * HD, (head + 1) * HD) for head in range(heads)]
        scores = [score(source_ref[:length, cols], query_ref[:, cols]) for cols in columns]
        rounded, kept = [], []
        for head in range(heads):
            top = jnp.maximum(top_ref[head], jnp.max(scores[head], axis=0, keepdims=True) + bias)
            weights = jnp.exp2(scores[head] - (top - bias))
            kept.append(jnp.exp2(top_ref[head] - top))
            new_top_ref[head] = top
            new_total_ref[head] = total_ref[head] * kept[head] + jnp.sum(weights, axis=0, keepdims=True)
            rounded.append(weights.astype(query_ref.dtype))
        for head, cols in enumerate(columns):
            new_part_ref[head] = part_ref[head] * kept[head] + weigh(source_ref[length:, cols], rounded[head])

    operands = [pltpu.with_memory_space_constraint(array, pltpu.VMEM) for array in (queries, source, *state)]
    return pl.pallas_call(
        kernel,
        name="join",
        compiler_params=ROOM,
        out_shape=state_shapes(heads, rows),
        in_specs=[IN_VMEM] * len(operands),
        out_specs=[IN_VMEM] * 3,
        cost_estimate=cost(rows, length, width),
    )(*operands)


def finish(queries, sources, choices, state, first, earlier):
    rows, width = queries.shape
    count = len(sources)
    lengths = [source.shape[0] // 2 for source in sources]
    heads = range(first, first + sources[-1].shape[1] // HD)
    whole = earlier is not None

    def columns(head):
        return slice(head * HD, (head + 1) * HD)

    def kernel(query_ref, *rest):
        source_refs, (top_ref, total_ref, part_ref, *rest) = rest[:count], rest[count:]
        if whole:
            earlier_ref, out_hbm, out_ref, sems = rest
            sent = [pltpu.make_async_copy(earlier_ref.at[head], out_hbm.at[:, columns(head)], sems.at[head]) for head in range(first)]
            for copy in sent:
                copy.start()
        else:
            (out_ref,), sent = rest, []
        biases = [jnp.where(either(choice, has_partner) == 1, 0.0, MASKED).astype(jnp.float32) for choice in choices]

        def held(head, values):
            cut = [columns(head if ref.shape[1] == width else head - first) for ref in source_refs]
            return [
                ref[length:, cols] if values else ref[:length, cols] for ref, length, cols in zip(source_refs, lengths, cut)
            ]

        def run(true_maximum, sent):
            scores = [[score(key, query_ref[:, columns(head)]) for key in held(head, False)] for head in heads]
            rounded, totals, before = [], [], []
            for head, parts in zip(heads, scores):
                top, total, part = top_ref[head], total_ref[head], part_ref[head]
                if true_maximum:
                    for scored, bias in zip(parts, biases):
                        top = jnp.maximum(top, jnp.max(scored, axis=0, keepdims=True) + bias)
                    kept = jnp.exp2(top_ref[head] - top)
                    total, part = total * kept, part * kept
                weights = [jnp.exp2(scored - (top - bias)) for scored, bias in zip(parts, biases)]
                totals.append(total + sum(jnp.sum(weight, axis=0, keepdims=True) for weight in weights))
                before.append(part)
                rounded.append(jnp.concatenate([weight.astype(query_ref.dtype) for weight in weights]))
            new = [weigh(jnp.concatenate(held(head, True)), weights) for head, weights in zip(heads, rounded)]
            copies = list(sent)
            for place, head in enumerate(heads):
                out_ref[place] = ((before[place] + new[place]) * (1.0 / totals[place])).astype(out_ref.dtype).T
                if whole:
                    copies.append(pltpu.make_async_copy(out_ref.at[place], out_hbm.at[:, columns(head)], sems.at[head]))
                    copies[-1].start()
            small = functools.reduce(jnp.logical_and, [total < SAFE_TOTAL for total in totals])
            far = jnp.max(jnp.where(small, 0, 1))
            for copy in copies:
                copy.wait()
            return far

        far = run(False, sent)

        @pl.when(far > 0)
        def _():
            run(True, [])

    given = (queries, *sources, *state, *([earlier] if whole else []))
    operands = [pltpu.with_memory_space_constraint(array, pltpu.VMEM) for array in given]
    out_ref = pltpu.VMEM((len(heads), rows, HD), queries.dtype)
    return pl.pallas_call(
        kernel,
        name="finish" if whole else "settle",
        compiler_params=ROOM,
        out_shape=pltpu.HBM((rows, width), queries.dtype) if whole else out_ref,
        in_specs=[IN_VMEM] * len(operands),
        out_specs=ANYWHERE if whole else IN_VMEM,
        scratch_shapes=[out_ref, pltpu.SemaphoreType.DMA((heads.stop,))] if whole else [],
        cost_estimate=cost(rows, sum(lengths), len(heads) * HD),
    )(*operands)


def per_device(queries, keys, values, adj_mask, border_blocks):
    queries, keys, values = queries[0, 0], keys[0, 0], values[0, 0]
    border_blocks = border_blocks[0, 0].T
    width = queries.shape[1]
    early = width // HD - width // HD // LAST_SHARE
    plan = swap_plan({axis: lax.axis_size(axis) for axis in AXES}, border_blocks.shape[0])
    cut = max(0, len(plan) - 2)
    pieces = [(slice(0, width),)] * cut + [(slice(0, early * HD), slice(early * HD, width))] * (len(plan) - cut)
    outgoing, keys, values = pick(plan, pieces, adj_mask[0, 0], border_blocks, keys, values)
    state = own(queries, keys, values)
    for number in range(2, len(plan)):
        outgoing[number], state = lax.optimization_barrier((outgoing[number], state))
    incoming = [[swap(rows, choice) for rows in parts] for parts, choice in zip(outgoing, plan)]
    last = max(0, len(plan) - LAST_SOURCES)
    for number in range(last):
        state = join(queries, incoming[number][0], plan[number], state)
    settled = finish(queries, [parts[0] for parts in incoming[last:]], plan[last:], state, 0, None)
    return finish(queries, [parts[-1] for parts in incoming[last:]], plan[last:], state, early, settled)[None, None]


def solution(mesh):
    wide = P(("clip", "tm"), "band", None, "head")
    narrow = P(("clip", "tm"), "band", None, None)
    return jax.shard_map(
        per_device, mesh=mesh, in_specs=(wide, wide, wide, narrow, narrow), out_specs=wide, check_vma=False
    )
```
